32 devices in a mesh: step: 4 (over y, x), seq: 8 (over z, core).
Axes of the slice: x: 2, y: 2, z: 4, core: 2. Of those that a mesh axis runs over, the one named last changes fastest.
Arguments:
- latents: float32 [4, 256, 64], P('step', 'seq'), may hold values from -6 to 6
- timesteps: int32 [5], replicated, may hold values from 0 to 1000, as said below
- embed_weight: bfloat16 [64, 4096], replicated, may hold values from -0.75 to 0.75
- mod_weight: float32 [256, 2, 4096], P('seq'), may hold values from -0.375 to 0.375
- qkv_weight: bfloat16 [4096, 8, 3, 128], P('step', 'seq'), may hold values from -0.09375 to 0.09375
- out_weight: bfloat16 [8, 128, 64], P('seq'), may hold values from -6 to 6
Outputs:
- updated: float32 [4, 256, 64], P('step', 'seq')
- velocity: float32 [4, 256, 64], P('step', 'seq')
The draws below stay inside these ranges and needn't reach their ends.
Inputs may be any that keep to these rules, and one draw needn't show every extreme that they name: `timesteps`: strictly decreasing along the table.
All inputs are finite; a program needn't handle non-finite values.
Results may differ from the reference program's by a relative error of at most 0.0049.
Values may be sent and summed in bfloat16 or wider, within the bound.
A program may use at most 64 MiB of HBM per device.

```python
import math
import jax
import jax.numpy as jnp
from jax import lax

D = 4096
HD = 128
C = 64
FREQ = 256
HEADS = 8
STEPS = 4
TOKENS = 256


def draw_timesteps(key, part):
    first_key, second_key = jax.random.split(jax.random.fold_in(key, 7))
    top_stamp = 1000 - jax.random.randint(first_key, (), 0, 40, dtype=jnp.int32)
    decrements = jax.random.randint(second_key, (STEPS,), 500 // STEPS, 900 // STEPS + 1, dtype=jnp.int32)
    cumulative = jnp.concatenate([jnp.zeros((1,), jnp.int32), jnp.cumsum(decrements).astype(jnp.int32)])
    return (top_stamp - cumulative).astype(jnp.int32)


def steps_of(own_key, shape, pieces, smallest, high):
    gain, own = 1.0, jax.random.fold_in(own_key, 6)
    for axis_at, parts in pieces:
        steps = jnp.exp(jax.random.uniform(jax.random.fold_in(own, axis_at), (parts,), jnp.float32, smallest / len(pieces), high / len(pieces)))
        gain = gain * jnp.repeat(steps, shape[axis_at] // parts).reshape([-1 if axis == axis_at else 1 for axis in range(len(shape))])
    return gain


def scatter_about(stream_key, dims, width, reach, shards=(), kind=jnp.bfloat16):
    level = steps_of(stream_key, dims, shards, -0.22, 0.18) if shards else 1.0
    entries = jax.random.normal(stream_key, dims, jnp.float32) * width * level
    return jnp.minimum(jnp.maximum(entries, -reach), reach).astype(kind)


def setup_inputs(seed: int = 0) -> dict:
    key_list = jax.random.split(jax.random.key(seed), 7)
    latents = scatter_about(key_list[0], (STEPS, TOKENS, C), 1.0, 6.0, ((0, 4), (1, 8)), jnp.float32)
    timesteps = draw_timesteps(jax.random.fold_in(key_list[6], 71), 0)
    embed_weight = scatter_about(key_list[2], (C, D), C ** -0.5, 0.75)
    mod_weight = scatter_about(key_list[3], (FREQ, 2, D), FREQ ** -0.5, 0.375, ((0, 8),), jnp.float32)
    qkv_weight = scatter_about(key_list[4], (D, HEADS, 3, HD), D ** -0.5, 0.09375, ((0, 4), (1, 8)))
    out_weight = scatter_about(key_list[5], (HEADS, HD, C), (1.2 * (TOKENS / (HEADS * HD)) ** 0.5), 6.0, ((0, 8),))
    return {"latents": latents, "timesteps": timesteps, "embed_weight": embed_weight, "mod_weight": mod_weight, "qkv_weight": qkv_weight, "out_weight": out_weight}


def condition_of(stamp):
    half_count = FREQ // 2
    frequencies = jnp.exp(-math.log(10000.0) * jnp.arange(half_count, dtype=jnp.float32) / half_count)
    angles = stamp * frequencies
    return jnp.concatenate([jnp.cos(angles), jnp.sin(angles)])

def modulate(latent_rows, embed_weight, shift_vec, scale_vec):
    embedded = jnp.dot(latent_rows, embed_weight, preferred_element_type=jnp.float32)
    center_mean = lax.optimization_barrier(jnp.mean(embedded, axis=-1, keepdims=True))
    centered = embedded - center_mean
    variance = lax.optimization_barrier(jnp.mean(centered * centered, axis=-1, keepdims=True))
    normed = centered * lax.rsqrt(variance + 1e-06)
    return (normed * (1.0 + shift_vec * 0.0 + scale_vec) + shift_vec).astype(jnp.bfloat16)

def qk_norm(head_rows):
    as_float = head_rows.astype(jnp.float32)
    return (as_float * lax.rsqrt(lax.optimization_barrier(jnp.mean(as_float * as_float, axis=-1, keepdims=True)) + 1e-06)).astype(jnp.bfloat16)

def attend_head(head_block):
    queries = qk_norm(head_block[:, 0])
    key_rows = qk_norm(head_block[:, 1])
    values = head_block[:, 2]
    seq_length = queries.shape[0]
    head_dim = queries.shape[1]
    block_rows = math.gcd(seq_length, 512)
    query_blocks = queries.reshape(seq_length // block_rows, block_rows, head_dim)

    def one_block(query_block):
        scores = jnp.dot(query_block, key_rows.T, preferred_element_type=jnp.float32) * (1.0 / math.sqrt(head_dim))
        weights = jnp.exp(scores)
        probabilities = (weights / lax.optimization_barrier(jnp.sum(weights, axis=-1, keepdims=True))).astype(jnp.bfloat16)
        return jnp.dot(probabilities, values, preferred_element_type=jnp.float32).astype(jnp.bfloat16)
    return lax.map(one_block, query_blocks).reshape(seq_length, head_dim)

def reference(latents, timesteps, embed_weight, mod_weight, qkv_weight, out_weight):
    stamps = timesteps.astype(jnp.float32)

    def one_step(inputs):
        latent_rows, stamp = inputs
        modulation = jnp.einsum('f,fcd->cd', condition_of(stamp), mod_weight, precision=lax.Precision.HIGHEST)
        modulated = modulate(latent_rows.astype(jnp.bfloat16), embed_weight, modulation[0], modulation[1])
        model_width = modulated.shape[1]
        seq_length = modulated.shape[0]
        projected = jnp.dot(modulated, qkv_weight.reshape(model_width, -1), preferred_element_type=jnp.float32)
        projected = projected.astype(jnp.bfloat16).reshape(seq_length, qkv_weight.shape[1], 3, qkv_weight.shape[3])
        attended = lax.map(attend_head, jnp.moveaxis(projected, 1, 0))
        return jnp.einsum('hsd,hdc->sc', attended.astype(jnp.float32), out_weight.astype(jnp.float32), precision=lax.Precision.HIGHEST)
    velocity = lax.map(one_step, (latents, stamps[:-1]))
    step_sizes = (stamps[1:] - stamps[:-1]) / 1000.0
    updated = latents[0][None] + jnp.cumsum(step_sizes[:, None, None] * velocity, axis=0)
    return (updated, velocity)
```

```python
import functools
import math

import jax
import jax.numpy as jnp
from jax import lax
from jax.experimental import pallas as pl
from jax.experimental.pallas import tpu as pltpu
from jax.sharding import PartitionSpec as P

FREQ = 256


def carried_in(shard, axis, combine, identity):
    devices, place = (lax.axis_size(axis), lax.axis_index(axis))
    everything = lax.all_gather(shard, axis)
    start = jnp.broadcast_to(jnp.asarray(identity, shard.dtype), shard.shape)

    def step(k, before):
        reached = k < place
        new = combine(before, everything[k])
        return jnp.where(reached, new, before)

    return lax.fori_loop(0, devices, step, start)


def condition_of(stamp):
    half_count = FREQ // 2
    frequencies = jnp.exp(
        -math.log(10000.0) * jnp.arange(half_count, dtype=jnp.float32) / half_count
    )
    angles = stamp * frequencies
    return jnp.concatenate([jnp.cos(angles), jnp.sin(angles)])


def modulate(latent_rows, embed_weight, shift_vec, scale_vec):
    embedded = jnp.dot(latent_rows, embed_weight, preferred_element_type=jnp.float32)
    center_mean = jnp.mean(embedded, axis=-1, keepdims=True)
    centered = embedded - center_mean
    variance = jnp.mean(centered * centered, axis=-1, keepdims=True)
    normed = centered * lax.rsqrt(variance + 1e-06)
    return (normed * (1.0 + scale_vec) + shift_vec).astype(jnp.bfloat16)


def qk_norm(head_rows):
    as_float = head_rows.astype(jnp.float32)
    return (
        as_float * lax.rsqrt(jnp.mean(as_float * as_float, axis=-1, keepdims=True) + 1e-06)
    ).astype(jnp.bfloat16)


def attend_head(head_block):
    queries = qk_norm(head_block[:, 0])
    key_rows = qk_norm(head_block[:, 1])
    values = head_block[:, 2]
    seq_length = queries.shape[0]
    head_dim = queries.shape[1]
    block_rows = math.gcd(seq_length, 512)
    query_blocks = queries.reshape(seq_length // block_rows, block_rows, head_dim)

    def one_block(query_block):
        scores = jnp.dot(query_block, key_rows.T, preferred_element_type=jnp.float32) * (
            1.0 / math.sqrt(head_dim)
        )
        weights = jnp.exp(scores)
        probabilities = (weights / jnp.sum(weights, axis=-1, keepdims=True)).astype(jnp.bfloat16)
        return jnp.dot(probabilities, values, preferred_element_type=jnp.float32).astype(
            jnp.bfloat16
        )

    return lax.map(one_block, query_blocks).reshape(seq_length, head_dim)


def add_terms(earlier_sum, later_sum):
    return earlier_sum + later_sum


def on_device(latents, timesteps, embed_weight, mod_weight, qkv_weight, out_weight):
    step_index = lax.axis_index("step")
    seq_index = lax.axis_index("seq")
    stamp_pair = lax.dynamic_slice_in_dim(timesteps, step_index, 2, 0).astype(jnp.float32)
    condition_vec = condition_of(stamp_pair[0])
    feature_rows = mod_weight.shape[0]
    local_features = lax.dynamic_slice_in_dim(
        condition_vec, seq_index * feature_rows, feature_rows, 0
    )
    partial_mod = jnp.einsum(
        "f,fcd->cd", local_features, mod_weight, precision=lax.Precision.HIGHEST
    )
    modulation = lax.psum(partial_mod, "seq")
    own_latents = latents[0].astype(jnp.bfloat16)
    all_latents = lax.all_gather(own_latents, "seq", axis=0, tiled=True)
    gathered = modulate(all_latents, embed_weight, modulation[0], modulation[1])
    seq_length = gathered.shape[0]
    heads_here = qkv_weight.shape[1]
    head_dim = qkv_weight.shape[3]
    qkv_width = heads_here * 3 * head_dim
    weight_piece = lax.all_gather(qkv_weight, "step", axis=0, tiled=True)
    flat_piece = weight_piece.reshape(weight_piece.shape[0], qkv_width)
    accumulated = jnp.dot(gathered, flat_piece, preferred_element_type=jnp.float32)
    projected = accumulated.astype(jnp.bfloat16).reshape(seq_length, heads_here, 3, head_dim)
    attended = lax.map(attend_head, jnp.moveaxis(projected, 1, 0))
    merged_heads = jnp.moveaxis(attended, 0, 1).reshape(seq_length, heads_here * head_dim)
    out_matrix = out_weight.reshape(heads_here * head_dim, out_weight.shape[2])
    velocity = lax.psum_scatter(
        jnp.dot(merged_heads, out_matrix, preferred_element_type=jnp.float32),
        "seq",
        scatter_dimension=0,
        tiled=True,
    )
    step_size = (stamp_pair[1] - stamp_pair[0]) / 1000.0
    increment = step_size * velocity + jnp.where(
        step_index == 0, latents[0], jnp.zeros_like(latents[0])
    )
    earlier = carried_in(increment, "step", add_terms, jnp.zeros_like(increment))
    updated = earlier + increment
    return (updated[None], velocity[None])


MESH = pl.DeviceIdType.MESH
ANY = pl.BlockSpec(memory_space=pl.ANY)
VMEM = pl.BlockSpec(memory_space=pltpu.VMEM)


def fused_kernel(
    steps, seqs, stamps, latents, embed_hbm, mod_hbm, qkv_hbm, out_hbm,
    updated, velocity,
    lat_v, embed, mod_v, weight, out_v,
    mod_part, mod_recv, mod_all, rows_all, lhs, fold_send, fold_recv,
    vel_send, vel_recv, inc_send, inc_recv,
    local_sem, a_send, a_get, b_send, b_get, x_send, x_get,
    m_send, m_get, v_send, v_get, i_send, i_get,
):
    j, s = lax.axis_index("step"), lax.axis_index("seq")
    rows, channels = lat_v.shape
    width = embed.shape[1]
    features = mod_hbm.shape[0]
    block = mod_v.shape[1]
    lanes = block // seqs
    fold_rows = fold_recv.shape[1]
    head_dim = out_v.shape[1]
    half = features * seqs // 2

    def seq_peer(i):
        return lax.rem(s + i, seqs)

    def step_peer(i):
        return lax.rem(j + i, steps)

    barrier = pltpu.get_barrier_semaphore()
    for i in range(1, seqs):
        pl.semaphore_signal(barrier, inc=1, device_id=(j, seq_peer(i)), device_id_type=MESH)
    for i in range(1, steps):
        pl.semaphore_signal(barrier, inc=1, device_id=(step_peer(i), s), device_id_type=MESH)

    own_columns = pl.ds(pl.multiple_of(j * block, block), block)
    loads = [
        pltpu.make_async_copy(
            mod_hbm.at[:, c, own_columns],
            mod_v.at[pl.ds(c * features, features), :],
            local_sem.at[c],
        )
        for c in range(2)
    ]
    load_lat = pltpu.make_async_copy(latents, lat_v, local_sem.at[2])
    load_embed = pltpu.make_async_copy(embed_hbm, embed, local_sem.at[3])
    load_weight = [
        pltpu.make_async_copy(
            qkv_hbm.at[c], weight.at[:, pl.ds(c * head_dim, head_dim)], local_sem.at[4 + c]
        )
        for c in range(3)
    ]
    load_out = pltpu.make_async_copy(out_hbm, out_v, local_sem.at[7])
    for copy in (*loads, load_lat, load_embed, *load_weight, load_out):
        copy.start()

    shape = (2 * steps, 2 * features)
    row = lax.broadcasted_iota(jnp.int32, shape, 0)
    column = lax.broadcasted_iota(jnp.int32, shape, 1)
    low_row, low_column = row < steps, column < features
    step_of = jnp.where(low_row, row, row - steps)
    feature = jnp.where(low_column, column, column - features) + s * features
    is_cos = feature < half
    index = jnp.where(is_cos, feature, feature - half)
    stamp = jnp.zeros(shape, jnp.float32)
    for k in range(steps):
        stamp = jnp.where(step_of == k, stamps[k].astype(jnp.float32), stamp)
    frequency = jnp.exp(-math.log(10000.0) * index.astype(jnp.float32) / half)
    angle = stamp * frequency
    condition = jnp.where(is_cos, jnp.cos(angle), jnp.sin(angle))
    condition = jnp.where(low_row == low_column, condition, 0.0)

    for copy in loads:
        copy.wait()
    part = jnp.dot(
        condition, mod_v[...], precision=lax.Precision.HIGHEST, preferred_element_type=jnp.float32
    )
    for q in range(seqs):
        mod_part[q] = part[:, q * lanes:(q + 1) * lanes]

    pl.semaphore_wait(barrier, seqs + steps - 2)

    def to_seq(i, src, dst, send, get):
        return pltpu.make_async_remote_copy(
            src_ref=src, dst_ref=dst, send_sem=send.at[i - 1], recv_sem=get.at[i - 1],
            device_id=(j, seq_peer(i)), device_id_type=MESH,
        )

    def to_step(i, src, dst, send, get):
        return pltpu.make_async_remote_copy(
            src_ref=src, dst_ref=dst, send_sem=send.at[i - 1], recv_sem=get.at[i - 1],
            device_id=(step_peer(i), s), device_id_type=MESH,
        )

    a_copies = [
        to_seq(i, mod_part.at[seq_peer(i)], mod_recv.at[i - 1], a_send, a_get)
        for i in range(1, seqs)
    ]
    for copy in a_copies:
        copy.start()

    load_lat.wait()
    load_embed.wait()
    own = lat_v[...].astype(jnp.bfloat16)
    embedded = jnp.dot(own, embed[...], preferred_element_type=jnp.float32)
    centered = embedded - jnp.mean(embedded, axis=-1, keepdims=True)
    scale = lax.rsqrt(jnp.mean(centered * centered, axis=-1, keepdims=True) + 1e-06)
    scale_high = scale.astype(jnp.bfloat16)
    scale_low = (scale - scale_high.astype(jnp.float32)).astype(jnp.bfloat16)
    rows_all[s] = jnp.concatenate(
        [
            own,
            jnp.broadcast_to(scale_high, (rows, channels // 2)),
            jnp.broadcast_to(scale_low, (rows, channels // 2)),
        ],
        axis=1,
    )
    x_copies = [
        to_seq(i, rows_all.at[s], rows_all.at[s], x_send, x_get) for i in range(1, seqs)
    ]
    for copy in x_copies:
        copy.start()

    total = mod_part[s]
    for i in range(1, seqs):
        a_copies[i - 1].wait_recv()
        total = total + mod_recv[i - 1]
    mod_all[s] = total
    b_copies = [
        to_seq(i, mod_all.at[s], mod_all.at[s], b_send, b_get) for i in range(1, seqs)
    ]
    for copy in b_copies:
        copy.start()

    embed_mean = jnp.mean(embed[...].astype(jnp.float32), axis=-1, keepdims=True)
    tail_row = lax.broadcasted_iota(jnp.int32, (fold_rows - channels, lanes), 0)
    for copy in b_copies:
        copy.wait_recv()
    for q in range(seqs):
        at = pl.ds(q * lanes, lanes)
        own_at = pl.ds(pl.multiple_of(j * block + q * lanes, lanes), lanes)
        embed_block = embed[:, own_at].astype(jnp.float32) - embed_mean
        for i in range(steps):
            k = step_peer(i)
            shift_k = mod_all[q, pl.ds(k, 1), :]
            scale_k = mod_all[q, pl.ds(steps + k, 1), :]
            lhs[pl.ds(i * fold_rows, channels), at] = (embed_block * (1.0 + scale_k)).astype(
                jnp.bfloat16
            )
            lhs[pl.ds(i * fold_rows + channels, fold_rows - channels), at] = jnp.where(
                tail_row == 0, shift_k, 0.0
            ).astype(jnp.bfloat16)

    for copy in load_weight:
        copy.wait()
    folded = jnp.dot(lhs[...], weight[...], preferred_element_type=jnp.float32)
    m_copies = []
    for i in range(1, steps):
        fold_send[i - 1] = folded[i * fold_rows:(i + 1) * fold_rows].astype(jnp.bfloat16)
        copy = to_step(i, fold_send.at[i - 1], fold_recv.at[i - 1], m_send, m_get)
        copy.start()
        m_copies.append(copy)
    for copy in x_copies:
        copy.wait_recv()
    tokens = rows_all[...].reshape(seqs * rows, 2 * channels)
    latent_rows = tokens[:, :channels]
    token_scale = tokens[:, channels:channels + 1].astype(jnp.float32) + tokens[
        :, channels + channels // 2:channels + channels // 2 + 1
    ].astype(jnp.float32)
    matrix = folded[:fold_rows]
    for i in range(1, steps):
        m_copies[i - 1].wait_recv()
        matrix = matrix + fold_recv[i - 1].astype(jnp.float32)
    main = matrix[:channels]
    main_high = main.astype(jnp.bfloat16)
    main_low = (main - main_high.astype(jnp.float32)).astype(jnp.bfloat16)
    projected = token_scale * (
        jnp.dot(latent_rows, main_high, preferred_element_type=jnp.float32)
        + jnp.dot(latent_rows, main_low, preferred_element_type=jnp.float32)
    ) + matrix[channels:channels + 1]
    projected = projected.astype(jnp.bfloat16)
    queries = qk_norm(projected[:, :head_dim])
    keys = qk_norm(projected[:, head_dim:2 * head_dim])
    values = projected[:, 2 * head_dim:]
    last = (((1,), (1,)), ((), ()))
    scores = lax.dot_general(queries, keys, last, preferred_element_type=jnp.float32)
    weights = jnp.exp(scores * (1.0 / math.sqrt(head_dim)))
    probabilities = (weights / jnp.sum(weights, axis=-1, keepdims=True)).astype(jnp.bfloat16)
    attended = jnp.dot(probabilities, values, preferred_element_type=jnp.float32).astype(
        jnp.bfloat16
    )
    load_out.wait()
    share = lax.dot_general(attended, out_v[...], last, preferred_element_type=jnp.float32)
    for q in range(seqs):
        vel_send[q] = share[q * rows:(q + 1) * rows]
    v_copies = [
        to_seq(i, vel_send.at[seq_peer(i)], vel_recv.at[i - 1], v_send, v_get)
        for i in range(1, seqs)
    ]
    for copy in v_copies:
        copy.start()
    speed = vel_send[s]
    for i in range(1, seqs):
        v_copies[i - 1].wait_recv()
        speed = speed + vel_recv[i - 1]
    velocity[...] = speed

    step_size = (stamps[j + 1].astype(jnp.float32) - stamps[j].astype(jnp.float32)) * 0.001
    increment = step_size * speed + jnp.where(j == 0, lat_v[...], 0.0)
    updated[...] = increment
    inc_send[...] = increment
    i_copies = [
        to_step(i, inc_send, inc_recv.at[i - 1], i_send, i_get) for i in range(1, steps)
    ]
    for i in range(1, steps):
        pl.when(j + i < steps)(i_copies[i - 1].start)
    for i in range(1, steps):
        @pl.when(j >= i)
        def _():
            i_copies[i - 1].wait_recv()
            updated[...] += inc_recv[i - 1]

    for copy in (*a_copies, *x_copies, *b_copies, *m_copies, *v_copies):
        copy.wait_send()
    for i in range(1, steps):
        pl.when(j + i < steps)(i_copies[i - 1].wait_send)


def fused(steps, seqs, latents, timesteps, embed_weight, mod_weight, qkv_weight, out_weight):
    _, rows, channels = latents.shape
    width = embed_weight.shape[1]
    features = mod_weight.shape[0]
    block, _, _, head_dim = qkv_weight.shape
    lanes = block // seqs
    fold_rows = channels + 16
    bf16, f32 = jnp.bfloat16, jnp.float32
    out_shape = jax.ShapeDtypeStruct((rows, channels), f32)
    dma = pltpu.SemaphoreType.DMA
    seq_sems = [dma((seqs - 1,))] * 2
    step_sems = [dma((steps - 1,))] * 2
    updated, velocity = pl.pallas_call(
        functools.partial(fused_kernel, steps, seqs),
        out_shape=(out_shape, out_shape),
        in_specs=[pl.BlockSpec(memory_space=pltpu.SMEM)] + [ANY] * 5,
        out_specs=(VMEM, VMEM),
        scratch_shapes=[
            pltpu.VMEM((rows, channels), f32),
            pltpu.VMEM((channels, width), bf16),
            pltpu.VMEM((2 * features, block), f32),
            pltpu.VMEM((block, 3 * head_dim), bf16),
            pltpu.VMEM((channels, head_dim), bf16),
            pltpu.VMEM((seqs, 2 * steps, lanes), f32),
            pltpu.VMEM((seqs - 1, 2 * steps, lanes), f32),
            pltpu.VMEM((seqs, 2 * steps, lanes), f32),
            pltpu.VMEM((seqs, rows, 2 * channels), bf16),
            pltpu.VMEM((steps * fold_rows, block), bf16),
            pltpu.VMEM((steps - 1, fold_rows, 3 * head_dim), bf16),
            pltpu.VMEM((steps - 1, fold_rows, 3 * head_dim), bf16),
            pltpu.VMEM((seqs, rows, channels), f32),
            pltpu.VMEM((seqs - 1, rows, channels), f32),
            pltpu.VMEM((rows, channels), f32),
            pltpu.VMEM((steps - 1, rows, channels), f32),
            dma((8,)),
            *seq_sems, *seq_sems, *seq_sems, *step_sems, *seq_sems, *step_sems,
        ],
        compiler_params=pltpu.CompilerParams(
            collective_id=0, has_side_effects=True, vmem_limit_bytes=32 * 1024 * 1024
        ),
    )(
        timesteps,
        latents[0],
        embed_weight,
        mod_weight,
        jnp.transpose(qkv_weight, (1, 2, 0, 3))[0],
        jnp.transpose(out_weight, (0, 2, 1))[0],
    )
    return updated[None], velocity[None]


def body(steps, seqs, latents, timesteps, embed_weight, mod_weight, qkv_weight, out_weight):
    block, heads_here, _, head_dim = qkv_weight.shape
    fits = (
        steps > 1
        and seqs > 1
        and latents.shape[0] == 1
        and heads_here == 1
        and steps % 4 == 0
        and head_dim % 128 == 0
        and block % (seqs * 128) == 0
        and latents.shape[1] % 16 == 0
        and latents.shape[2] % 16 == 0
        and mod_weight.shape[0] % 8 == 0
    )
    run = functools.partial(fused, steps, seqs) if fits else on_device
    return run(latents, timesteps, embed_weight, mod_weight, qkv_weight, out_weight)


def solution(mesh):
    in_specs = (
        P("step", "seq", None),
        P(),
        P(),
        P("seq", None, None),
        P("step", "seq", None, None),
        P("seq", None, None),
    )
    out_specs = (P("step", "seq", None), P("step", "seq", None))
    return jax.shard_map(
        functools.partial(body, mesh.shape["step"], mesh.shape["seq"]), mesh=mesh, in_specs=in_specs, out_specs=out_specs, check_vma=False
    )
```

```python
import functools
import math

import jax
import jax.numpy as jnp
from jax import lax
from jax.experimental import pallas as pl
from jax.experimental.pallas import tpu as pltpu
from jax.sharding import PartitionSpec as P

FREQ = 256


def carried_in(shard, axis, combine, identity):
    devices, place = (lax.axis_size(axis), lax.axis_index(axis))
    everything = lax.all_gather(shard, axis)
    start = jnp.broadcast_to(jnp.asarray(identity, shard.dtype), shard.shape)

    def step(k, before):
        reached = k < place
        new = combine(before, everything[k])
        return jnp.where(reached, new, before)

    return lax.fori_loop(0, devices, step, start)


def condition_of(stamp):
    half_count = FREQ // 2
    frequencies = jnp.exp(
        -math.log(10000.0) * jnp.arange(half_count, dtype=jnp.float32) / half_count
    )
    angles = stamp * frequencies
    return jnp.concatenate([jnp.cos(angles), jnp.sin(angles)])


def modulate(latent_rows, embed_weight, shift_vec, scale_vec):
    embedded = jnp.dot(latent_rows, embed_weight, preferred_element_type=jnp.float32)
    center_mean = jnp.mean(embedded, axis=-1, keepdims=True)
    centered = embedded - center_mean
    variance = jnp.mean(centered * centered, axis=-1, keepdims=True)
    normed = centered * lax.rsqrt(variance + 1e-06)
    return (normed * (1.0 + scale_vec) + shift_vec).astype(jnp.bfloat16)


def qk_norm(head_rows):
    as_float = head_rows.astype(jnp.float32)
    return (
        as_float * lax.rsqrt(jnp.mean(as_float * as_float, axis=-1, keepdims=True) + 1e-06)
    ).astype(jnp.bfloat16)


def attend_head(head_block):
    queries = qk_norm(head_block[:, 0])
    key_rows = qk_norm(head_block[:, 1])
    values = head_block[:, 2]
    seq_length = queries.shape[0]
    head_dim = queries.shape[1]
    block_rows = math.gcd(seq_length, 512)
    query_blocks = queries.reshape(seq_length // block_rows, block_rows, head_dim)

    def one_block(query_block):
        scores = jnp.dot(query_block, key_rows.T, preferred_element_type=jnp.float32) * (
            1.0 / math.sqrt(head_dim)
        )
        weights = jnp.exp(scores)
        probabilities = (weights / jnp.sum(weights, axis=-1, keepdims=True)).astype(jnp.bfloat16)
        return jnp.dot(probabilities, values, preferred_element_type=jnp.float32).astype(
            jnp.bfloat16
        )

    return lax.map(one_block, query_blocks).reshape(seq_length, head_dim)


def add_terms(earlier_sum, later_sum):
    return earlier_sum + later_sum


def on_device(latents, timesteps, embed_weight, mod_weight, qkv_weight, out_weight):
    step_index = lax.axis_index("step")
    seq_index = lax.axis_index("seq")
    stamp_pair = lax.dynamic_slice_in_dim(timesteps, step_index, 2, 0).astype(jnp.float32)
    condition_vec = condition_of(stamp_pair[0])
    feature_rows = mod_weight.shape[0]
    local_features = lax.dynamic_slice_in_dim(
        condition_vec, seq_index * feature_rows, feature_rows, 0
    )
    partial_mod = jnp.einsum(
        "f,fcd->cd", local_features, mod_weight, precision=lax.Precision.HIGHEST
    )
    modulation = lax.psum(partial_mod, "seq")
    own_latents = latents[0].astype(jnp.bfloat16)
    all_latents = lax.all_gather(own_latents, "seq", axis=0, tiled=True)
    gathered = modulate(all_latents, embed_weight, modulation[0], modulation[1])
    seq_length = gathered.shape[0]
    heads_here = qkv_weight.shape[1]
    head_dim = qkv_weight.shape[3]
    qkv_width = heads_here * 3 * head_dim
    weight_piece = lax.all_gather(qkv_weight, "step", axis=0, tiled=True)
    flat_piece = weight_piece.reshape(weight_piece.shape[0], qkv_width)
    accumulated = jnp.dot(gathered, flat_piece, preferred_element_type=jnp.float32)
    projected = accumulated.astype(jnp.bfloat16).reshape(seq_length, heads_here, 3, head_dim)
    attended = lax.map(attend_head, jnp.moveaxis(projected, 1, 0))
    merged_heads = jnp.moveaxis(attended, 0, 1).reshape(seq_length, heads_here * head_dim)
    out_matrix = out_weight.reshape(heads_here * head_dim, out_weight.shape[2])
    velocity = lax.psum_scatter(
        jnp.dot(merged_heads, out_matrix, preferred_element_type=jnp.float32),
        "seq",
        scatter_dimension=0,
        tiled=True,
    )
    step_size = (stamp_pair[1] - stamp_pair[0]) / 1000.0
    increment = step_size * velocity + jnp.where(
        step_index == 0, latents[0], jnp.zeros_like(latents[0])
    )
    earlier = carried_in(increment, "step", add_terms, jnp.zeros_like(increment))
    updated = earlier + increment
    return (updated[None], velocity[None])


MESH = pl.DeviceIdType.MESH
HBM = pl.BlockSpec(memory_space=pltpu.HBM)
VMEM = pl.BlockSpec(memory_space=pltpu.VMEM)


def fused_kernel(
    steps, seqs, stamps, latents, embed_hbm, mod_hbm, qkv_hbm, out_hbm,
    result,
    lat_v, embed, mod_v, weight, out_v,
    mod_part, mod_recv, mod_all, rows_all, embed_own, lhs, fold_send, fold_recv,
    vel_send, vel_recv, inc_send, inc_recv,
    local_sem, a_send, a_get, b_send, b_get, x_send, x_get,
    m_send, m_get, v_send, v_get, i_send, i_get,
):
    j, s = lax.axis_index("step"), lax.axis_index("seq")
    rows, channels = lat_v.shape
    width = embed.shape[1]
    features = mod_hbm.shape[0]
    block = mod_v.shape[1]
    lanes = block // seqs
    fold_rows = fold_recv.shape[1]
    head_dim = out_v.shape[1]
    half = features * seqs // 2

    def seq_peer(i):
        return lax.rem(s + i, seqs)

    def step_peer(i):
        return lax.rem(j + i, steps)

    barrier = pltpu.get_barrier_semaphore()
    for i in range(1, seqs):
        pl.semaphore_signal(barrier, inc=1, device_id=(j, seq_peer(i)), device_id_type=MESH)
    for i in range(1, steps):
        pl.semaphore_signal(barrier, inc=1, device_id=(step_peer(i), s), device_id_type=MESH)

    own_columns = pl.ds(pl.multiple_of(j * block, block), block)
    loads = [
        pltpu.make_async_copy(
            mod_hbm.at[:, c, own_columns],
            mod_v.at[pl.ds(c * features, features), :],
            local_sem.at[c],
        )
        for c in range(2)
    ]
    load_lat = pltpu.make_async_copy(latents, lat_v, local_sem.at[2])
    load_embed = pltpu.make_async_copy(embed_hbm, embed, local_sem.at[3])
    load_weight = [
        pltpu.make_async_copy(
            qkv_hbm.at[c], weight.at[:, pl.ds(c * head_dim, head_dim)], local_sem.at[4 + c]
        )
        for c in range(3)
    ]
    load_out = pltpu.make_async_copy(out_hbm, out_v, local_sem.at[7])
    for copy in (*loads, load_lat, load_embed, *load_weight, load_out):
        copy.start()

    shape = (2 * steps, 2 * features)
    row = lax.broadcasted_iota(jnp.int32, shape, 0)
    column = lax.broadcasted_iota(jnp.int32, shape, 1)
    low_row, low_column = row < steps, column < features
    step_of = jnp.where(low_row, row, row - steps)
    feature = jnp.where(low_column, column, column - features) + s * features
    is_cos = feature < half
    index = jnp.where(is_cos, feature, feature - half)
    stamp = jnp.zeros(shape, jnp.float32)
    for k in range(steps):
        stamp = jnp.where(step_of == k, stamps[k].astype(jnp.float32), stamp)
    frequency = jnp.exp(-math.log(10000.0) * index.astype(jnp.float32) / half)
    angle = stamp * frequency
    condition = jnp.where(is_cos, jnp.cos(angle), jnp.sin(angle))
    condition = jnp.where(low_row == low_column, condition, 0.0)

    for copy in loads:
        copy.wait()
    part = jnp.dot(
        condition, mod_v[...], precision=lax.Precision.HIGHEST, preferred_element_type=jnp.float32
    )
    for q in range(seqs):
        mod_part[q] = part[:, q * lanes:(q + 1) * lanes]

    pl.semaphore_wait(barrier, seqs + steps - 2)

    def to_seq(i, src, dst, send, get):
        return pltpu.make_async_remote_copy(
            src_ref=src, dst_ref=dst, send_sem=send.at[i - 1], recv_sem=get.at[i - 1],
            device_id=(j, seq_peer(i)), device_id_type=MESH,
        )

    def to_step(i, src, dst, send, get):
        return pltpu.make_async_remote_copy(
            src_ref=src, dst_ref=dst, send_sem=send.at[i - 1], recv_sem=get.at[i - 1],
            device_id=(step_peer(i), s), device_id_type=MESH,
        )

    a_copies = [
        to_seq(i, mod_part.at[seq_peer(i)], mod_recv.at[i - 1], a_send, a_get)
        for i in range(1, seqs)
    ]
    for copy in a_copies:
        copy.start()

    load_lat.wait()
    load_embed.wait()
    own = lat_v[...].astype(jnp.bfloat16)
    embedded = jnp.dot(own, embed[...], preferred_element_type=jnp.float32)
    centered = embedded - jnp.mean(embedded, axis=-1, keepdims=True)
    scale = lax.rsqrt(jnp.mean(centered * centered, axis=-1, keepdims=True) + 1e-06)
    scale_high = scale.astype(jnp.bfloat16)
    scale_low = (scale - scale_high.astype(jnp.float32)).astype(jnp.bfloat16)
    rows_all[s] = jnp.concatenate(
        [
            own,
            jnp.broadcast_to(scale_high, (rows, channels // 2)),
            jnp.broadcast_to(scale_low, (rows, channels // 2)),
        ],
        axis=1,
    )
    x_copies = [
        to_seq(i, rows_all.at[s], rows_all.at[s], x_send, x_get) for i in range(1, seqs)
    ]
    for copy in x_copies:
        copy.start()

    total = mod_part[s]
    for i in range(1, seqs):
        a_copies[i - 1].wait_recv()
        total = total + mod_recv[i - 1]
    mod_all[s] = total
    b_copies = [
        to_seq(i, mod_all.at[s], mod_all.at[s], b_send, b_get) for i in range(1, seqs)
    ]
    for copy in b_copies:
        copy.start()

    embed_mean = jnp.mean(embed[...].astype(jnp.float32), axis=-1, keepdims=True)
    embed_own[...] = embed[:, own_columns].astype(jnp.float32) - embed_mean
    tail_row = lax.broadcasted_iota(jnp.int32, (fold_rows - channels, lanes), 0)
    for copy in b_copies:
        copy.wait_recv()
    for q in range(seqs):
        at = pl.ds(q * lanes, lanes)
        embed_block = embed_own[:, at]
        for i in range(steps):
            k = step_peer(i)
            shift_k = mod_all[q, pl.ds(k, 1), :]
            scale_k = mod_all[q, pl.ds(steps + k, 1), :]
            lhs[pl.ds(i * fold_rows, channels), at] = (embed_block * (1.0 + scale_k)).astype(
                jnp.bfloat16
            )
            lhs[pl.ds(i * fold_rows + channels, fold_rows - channels), at] = jnp.where(
                tail_row == 0, shift_k, 0.0
            ).astype(jnp.bfloat16)

    for copy in load_weight:
        copy.wait()
    folded = jnp.dot(lhs[...], weight[...], preferred_element_type=jnp.float32)
    m_copies = []
    for i in range(1, steps):
        fold_send[i - 1] = folded[i * fold_rows:(i + 1) * fold_rows].astype(jnp.bfloat16)
        copy = to_step(i, fold_send.at[i - 1], fold_recv.at[i - 1], m_send, m_get)
        copy.start()
        m_copies.append(copy)
    for copy in x_copies:
        copy.wait_recv()
    tokens = rows_all[...].reshape(seqs * rows, 2 * channels)
    latent_rows = tokens[:, :channels]
    token_scale = tokens[:, channels:channels + 1].astype(jnp.float32) + tokens[
        :, channels + channels // 2:channels + channels // 2 + 1
    ].astype(jnp.float32)
    matrix = folded[:fold_rows]
    for i in range(1, steps):
        m_copies[i - 1].wait_recv()
        matrix = matrix + fold_recv[i - 1].astype(jnp.float32)
    main = matrix[:channels]
    main_high = main.astype(jnp.bfloat16)
    main_low = (main - main_high.astype(jnp.float32)).astype(jnp.bfloat16)
    projected = token_scale * (
        jnp.dot(latent_rows, main_high, preferred_element_type=jnp.float32)
        + jnp.dot(latent_rows, main_low, preferred_element_type=jnp.float32)
    ) + matrix[channels:channels + 1]
    projected = projected.astype(jnp.bfloat16)
    queries = qk_norm(projected[:, :head_dim])
    keys = qk_norm(projected[:, head_dim:2 * head_dim])
    values = projected[:, 2 * head_dim:]
    last = (((1,), (1,)), ((), ()))
    scores = lax.dot_general(queries, keys, last, preferred_element_type=jnp.float32)
    weights = jnp.exp(scores * (1.0 / math.sqrt(head_dim)))
    probabilities = (weights / jnp.sum(weights, axis=-1, keepdims=True)).astype(jnp.bfloat16)
    attended = jnp.dot(probabilities, values, preferred_element_type=jnp.float32).astype(
        jnp.bfloat16
    )
    load_out.wait()
    share = lax.dot_general(attended, out_v[...], last, preferred_element_type=jnp.float32)
    for q in range(seqs):
        vel_send[q] = share[q * rows:(q + 1) * rows]
    v_copies = [
        to_seq(i, vel_send.at[seq_peer(i)], vel_recv.at[i - 1], v_send, v_get)
        for i in range(1, seqs)
    ]
    for copy in v_copies:
        copy.start()
    speed = vel_send[s]
    for i in range(1, seqs):
        v_copies[i - 1].wait_recv()
        speed = speed + vel_recv[i - 1]
    result[:, channels:] = speed

    step_size = (stamps[j + 1].astype(jnp.float32) - stamps[j].astype(jnp.float32)) * 0.001
    increment = step_size * speed + jnp.where(j == 0, lat_v[...], 0.0)
    result[:, :channels] = increment
    inc_send[...] = increment
    i_copies = [
        to_step(i, inc_send, inc_recv.at[i - 1], i_send, i_get) for i in range(1, steps)
    ]
    for i in range(1, steps):
        pl.when(j + i < steps)(i_copies[i - 1].start)
    for i in range(1, steps):
        @pl.when(j >= i)
        def _():
            i_copies[i - 1].wait_recv()
            result[:, :channels] += inc_recv[i - 1]

    for copy in (*a_copies, *x_copies, *b_copies, *m_copies, *v_copies):
        copy.wait_send()
    for i in range(1, steps):
        pl.when(j + i < steps)(i_copies[i - 1].wait_send)


def fused(steps, seqs, latents, timesteps, embed_weight, mod_weight, qkv_weight, out_weight):
    _, rows, channels = latents.shape
    width = embed_weight.shape[1]
    features = mod_weight.shape[0]
    block, _, _, head_dim = qkv_weight.shape
    lanes = block // seqs
    fold_rows = channels + 16
    bf16, f32 = jnp.bfloat16, jnp.float32
    out_shape = jax.ShapeDtypeStruct((rows, 2 * channels), f32)
    dma = pltpu.SemaphoreType.DMA
    seq_sems = [dma((seqs - 1,))] * 2
    step_sems = [dma((steps - 1,))] * 2
    result = pl.pallas_call(
        functools.partial(fused_kernel, steps, seqs),
        out_shape=out_shape,
        in_specs=[pl.BlockSpec(memory_space=pltpu.SMEM)] + [HBM] * 5,
        out_specs=VMEM,
        scratch_shapes=[
            pltpu.VMEM((rows, channels), f32),
            pltpu.VMEM((channels, width), bf16),
            pltpu.VMEM((2 * features, block), f32),
            pltpu.VMEM((block, 3 * head_dim), bf16),
            pltpu.VMEM((channels, head_dim), bf16),
            pltpu.VMEM((seqs, 2 * steps, lanes), f32),
            pltpu.VMEM((seqs - 1, 2 * steps, lanes), f32),
            pltpu.VMEM((seqs, 2 * steps, lanes), f32),
            pltpu.VMEM((seqs, rows, 2 * channels), bf16),
            pltpu.VMEM((channels, block), f32),
            pltpu.VMEM((steps * fold_rows, block), bf16),
            pltpu.VMEM((steps - 1, fold_rows, 3 * head_dim), bf16),
            pltpu.VMEM((steps - 1, fold_rows, 3 * head_dim), bf16),
            pltpu.VMEM((seqs, rows, channels), f32),
            pltpu.VMEM((seqs - 1, rows, channels), f32),
            pltpu.VMEM((rows, channels), f32),
            pltpu.VMEM((steps - 1, rows, channels), f32),
            dma((8,)),
            *seq_sems, *seq_sems, *seq_sems, *step_sems, *seq_sems, *step_sems,
        ],
        compiler_params=pltpu.CompilerParams(
            collective_id=0, has_side_effects=True, vmem_limit_bytes=56 * 1024 * 1024
        ),
    )(
        timesteps,
        latents[0],
        embed_weight,
        mod_weight,
        jnp.transpose(qkv_weight, (1, 2, 0, 3))[0],
        jnp.transpose(out_weight, (0, 2, 1))[0],
    )
    return result[None, :, :channels], result[None, :, channels:]


def body(steps, seqs, latents, timesteps, embed_weight, mod_weight, qkv_weight, out_weight):
    block, heads_here, _, head_dim = qkv_weight.shape
    fits = (
        steps > 1
        and seqs > 1
        and latents.shape[0] == 1
        and heads_here == 1
        and steps % 4 == 0
        and head_dim % 128 == 0
        and block % (seqs * 128) == 0
        and latents.shape[1] % 16 == 0
        and latents.shape[2] % 16 == 0
        and mod_weight.shape[0] % 8 == 0
    )
    run = functools.partial(fused, steps, seqs) if fits else on_device
    return run(latents, timesteps, embed_weight, mod_weight, qkv_weight, out_weight)


def solution(mesh):
    in_specs = (
        P("step", "seq", None),
        P(),
        P(),
        P("seq", None, None),
        P("step", "seq", None, None),
        P("seq", None, None),
    )
    out_specs = (P("step", "seq", None), P("step", "seq", None))
    return jax.shard_map(
        functools.partial(body, mesh.shape["step"], mesh.shape["seq"]), mesh=mesh, in_specs=in_specs, out_specs=out_specs, check_vma=False
    )
```

```python
import functools
import math

import jax
import jax.numpy as jnp
from jax import lax
from jax.experimental import pallas as pl
from jax.experimental.pallas import tpu as pltpu
from jax.sharding import PartitionSpec as P

FREQ = 256


def carried_in(shard, axis, combine, identity):
    devices, place = (lax.axis_size(axis), lax.axis_index(axis))
    everything = lax.all_gather(shard, axis)
    start = jnp.broadcast_to(jnp.asarray(identity, shard.dtype), shard.shape)

    def step(k, before):
        reached = k < place
        new = combine(before, everything[k])
        return jnp.where(reached, new, before)

    return lax.fori_loop(0, devices, step, start)


def condition_of(stamp):
    half_count = FREQ // 2
    frequencies = jnp.exp(
        -math.log(10000.0) * jnp.arange(half_count, dtype=jnp.float32) / half_count
    )
    angles = stamp * frequencies
    return jnp.concatenate([jnp.cos(angles), jnp.sin(angles)])


def modulate(latent_rows, embed_weight, shift_vec, scale_vec):
    embedded = jnp.dot(latent_rows, embed_weight, preferred_element_type=jnp.float32)
    center_mean = jnp.mean(embedded, axis=-1, keepdims=True)
    centered = embedded - center_mean
    variance = jnp.mean(centered * centered, axis=-1, keepdims=True)
    normed = centered * lax.rsqrt(variance + 1e-06)
    return (normed * (1.0 + scale_vec) + shift_vec).astype(jnp.bfloat16)


def qk_norm(head_rows):
    as_float = head_rows.astype(jnp.float32)
    return (
        as_float * lax.rsqrt(jnp.mean(as_float * as_float, axis=-1, keepdims=True) + 1e-06)
    ).astype(jnp.bfloat16)


def attend_head(head_block):
    queries = qk_norm(head_block[:, 0])
    key_rows = qk_norm(head_block[:, 1])
    values = head_block[:, 2]
    seq_length = queries.shape[0]
    head_dim = queries.shape[1]
    block_rows = math.gcd(seq_length, 512)
    query_blocks = queries.reshape(seq_length // block_rows, block_rows, head_dim)

    def one_block(query_block):
        scores = jnp.dot(query_block, key_rows.T, preferred_element_type=jnp.float32) * (
            1.0 / math.sqrt(head_dim)
        )
        weights = jnp.exp(scores)
        probabilities = (weights / jnp.sum(weights, axis=-1, keepdims=True)).astype(jnp.bfloat16)
        return jnp.dot(probabilities, values, preferred_element_type=jnp.float32).astype(
            jnp.bfloat16
        )

    return lax.map(one_block, query_blocks).reshape(seq_length, head_dim)


def add_terms(earlier_sum, later_sum):
    return earlier_sum + later_sum


def on_device(latents, timesteps, embed_weight, mod_weight, qkv_weight, out_weight):
    step_index = lax.axis_index("step")
    seq_index = lax.axis_index("seq")
    stamp_pair = lax.dynamic_slice_in_dim(timesteps, step_index, 2, 0).astype(jnp.float32)
    condition_vec = condition_of(stamp_pair[0])
    feature_rows = mod_weight.shape[0]
    local_features = lax.dynamic_slice_in_dim(
        condition_vec, seq_index * feature_rows, feature_rows, 0
    )
    partial_mod = jnp.einsum(
        "f,fcd->cd", local_features, mod_weight, precision=lax.Precision.HIGHEST
    )
    modulation = lax.psum(partial_mod, "seq")
    own_latents = latents[0].astype(jnp.bfloat16)
    all_latents = lax.all_gather(own_latents, "seq", axis=0, tiled=True)
    gathered = modulate(all_latents, embed_weight, modulation[0], modulation[1])
    seq_length = gathered.shape[0]
    heads_here = qkv_weight.shape[1]
    head_dim = qkv_weight.shape[3]
    qkv_width = heads_here * 3 * head_dim
    weight_piece = lax.all_gather(qkv_weight, "step", axis=0, tiled=True)
    flat_piece = weight_piece.reshape(weight_piece.shape[0], qkv_width)
    accumulated = jnp.dot(gathered, flat_piece, preferred_element_type=jnp.float32)
    projected = accumulated.astype(jnp.bfloat16).reshape(seq_length, heads_here, 3, head_dim)
    attended = lax.map(attend_head, jnp.moveaxis(projected, 1, 0))
    merged_heads = jnp.moveaxis(attended, 0, 1).reshape(seq_length, heads_here * head_dim)
    out_matrix = out_weight.reshape(heads_here * head_dim, out_weight.shape[2])
    velocity = lax.psum_scatter(
        jnp.dot(merged_heads, out_matrix, preferred_element_type=jnp.float32),
        "seq",
        scatter_dimension=0,
        tiled=True,
    )
    step_size = (stamp_pair[1] - stamp_pair[0]) / 1000.0
    increment = step_size * velocity + jnp.where(
        step_index == 0, latents[0], jnp.zeros_like(latents[0])
    )
    earlier = carried_in(increment, "step", add_terms, jnp.zeros_like(increment))
    updated = earlier + increment
    return (updated[None], velocity[None])


MESH = pl.DeviceIdType.MESH
HBM = pl.BlockSpec(memory_space=pltpu.HBM)
VMEM = pl.BlockSpec(memory_space=pltpu.VMEM)


def fused_kernel(
    steps, seqs, stamps, latents, embed_hbm, mod_hbm, qkv_hbm, out_hbm,
    result,
    lat_v, embed, mod_v, weight, out_v,
    mod_part, mod_recv, mod_all, rows_all, embed_own, lhs, fold_send, fold_recv,
    vel_send, vel_recv, inc_send, inc_recv,
    local_sem, a_send, a_get, b_send, b_get, x_send, x_get,
    m_send, m_get, v_send, v_get, i_send, i_get,
):
    j, s = lax.axis_index("step"), lax.axis_index("seq")
    rows, channels = lat_v.shape
    width = embed.shape[1]
    features = mod_hbm.shape[0]
    block = mod_v.shape[1]
    lanes = block // seqs
    fold_rows = fold_recv.shape[1]
    head_dim = out_v.shape[1]
    half = features * seqs // 2

    def seq_peer(i):
        return lax.rem(s + i, seqs)

    def step_peer(i):
        return lax.rem(j + i, steps)

    barrier = pltpu.get_barrier_semaphore()
    for i in range(1, seqs):
        pl.semaphore_signal(barrier, inc=1, device_id=(j, seq_peer(i)), device_id_type=MESH)
    for i in range(1, steps):
        pl.semaphore_signal(barrier, inc=1, device_id=(step_peer(i), s), device_id_type=MESH)

    own_columns = pl.ds(pl.multiple_of(j * block, block), block)
    loads = [
        pltpu.make_async_copy(
            mod_hbm.at[:, c, own_columns],
            mod_v.at[pl.ds(c * features, features), :],
            local_sem.at[c],
        )
        for c in range(2)
    ]
    load_lat = pltpu.make_async_copy(latents, lat_v, local_sem.at[2])
    load_embed = pltpu.make_async_copy(embed_hbm, embed, local_sem.at[3])
    load_weight = [
        pltpu.make_async_copy(
            qkv_hbm.at[c], weight.at[:, pl.ds(c * head_dim, head_dim)], local_sem.at[4 + c]
        )
        for c in range(3)
    ]
    load_out = pltpu.make_async_copy(out_hbm, out_v, local_sem.at[7])
    for copy in (*loads, load_lat, load_embed, *load_weight, load_out):
        copy.start()

    shape = (2 * steps, 2 * features)
    row = lax.broadcasted_iota(jnp.int32, shape, 0)
    column = lax.broadcasted_iota(jnp.int32, shape, 1)
    low_row, low_column = row < steps, column < features
    step_of = jnp.where(low_row, row, row - steps)
    feature = jnp.where(low_column, column, column - features) + s * features
    is_cos = feature < half
    index = jnp.where(is_cos, feature, feature - half)
    stamp = jnp.zeros(shape, jnp.float32)
    for k in range(steps):
        stamp = jnp.where(step_of == k, stamps[k].astype(jnp.float32), stamp)
    frequency = jnp.exp(-math.log(10000.0) * index.astype(jnp.float32) / half)
    angle = stamp * frequency
    condition = jnp.where(is_cos, jnp.cos(angle), jnp.sin(angle))
    condition = jnp.where(low_row == low_column, condition, 0.0)

    for copy in loads:
        copy.wait()
    part = jnp.dot(
        condition, mod_v[...], precision=lax.Precision.HIGHEST, preferred_element_type=jnp.float32
    )
    for q in range(seqs):
        mod_part[q] = part[:, q * lanes:(q + 1) * lanes]

    pl.semaphore_wait(barrier, seqs + steps - 2)

    def to_seq(i, src, dst, send, get):
        return pltpu.make_async_remote_copy(
            src_ref=src, dst_ref=dst, send_sem=send.at[i - 1], recv_sem=get.at[i - 1],
            device_id=(j, seq_peer(i)), device_id_type=MESH,
        )

    def to_step(i, src, dst, send, get):
        return pltpu.make_async_remote_copy(
            src_ref=src, dst_ref=dst, send_sem=send.at[i - 1], recv_sem=get.at[i - 1],
            device_id=(step_peer(i), s), device_id_type=MESH,
        )

    a_copies = [
        to_seq(i, mod_part.at[seq_peer(i)], mod_recv.at[i - 1], a_send, a_get)
        for i in range(1, seqs)
    ]
    for copy in a_copies:
        copy.start()

    load_lat.wait()
    load_embed.wait()
    own = lat_v[...].astype(jnp.bfloat16)
    embedded = jnp.dot(own, embed[...], preferred_element_type=jnp.float32)
    centered = embedded - jnp.mean(embedded, axis=-1, keepdims=True)
    scale = lax.rsqrt(jnp.mean(centered * centered, axis=-1, keepdims=True) + 1e-06)
    scale_high = scale.astype(jnp.bfloat16)
    scale_low = (scale - scale_high.astype(jnp.float32)).astype(jnp.bfloat16)
    rows_all[s] = jnp.concatenate(
        [
            own,
            jnp.broadcast_to(scale_high, (rows, channels // 2)),
            jnp.broadcast_to(scale_low, (rows, channels // 2)),
        ],
        axis=1,
    )

    total = mod_part[s]
    for i in range(1, seqs):
        a_copies[i - 1].wait_recv()
        total = total + mod_recv[i - 1]
    mod_all[s] = total
    b_copies = [
        to_seq(i, mod_all.at[s], mod_all.at[s], b_send, b_get) for i in range(1, seqs)
    ]
    for copy in b_copies:
        copy.start()
    x_copies = [
        to_seq(i, rows_all.at[s], rows_all.at[s], x_send, x_get) for i in range(1, seqs)
    ]
    for copy in x_copies:
        copy.start()

    embed_mean = jnp.mean(embed[...].astype(jnp.float32), axis=-1, keepdims=True)
    embed_own[...] = embed[:, own_columns].astype(jnp.float32) - embed_mean
    tail_row = lax.broadcasted_iota(jnp.int32, (fold_rows - channels, lanes), 0)
    for copy in b_copies:
        copy.wait_recv()
    for copy in load_weight:
        copy.wait()

    def fold(i):
        k = step_peer(i)
        for q in range(seqs):
            at = pl.ds(q * lanes, lanes)
            shift_k = mod_all[q, pl.ds(k, 1), :]
            scale_k = mod_all[q, pl.ds(steps + k, 1), :]
            lhs[pl.ds(i * fold_rows, channels), at] = (
                embed_own[:, at] * (1.0 + scale_k)
            ).astype(jnp.bfloat16)
            lhs[pl.ds(i * fold_rows + channels, fold_rows - channels), at] = jnp.where(
                tail_row == 0, shift_k, 0.0
            ).astype(jnp.bfloat16)
        return jnp.dot(
            lhs[pl.ds(i * fold_rows, fold_rows), :], weight[...],
            preferred_element_type=jnp.float32,
        )

    m_copies = []
    for i in range(1, steps):
        fold_send[i - 1] = fold(i).astype(jnp.bfloat16)
        copy = to_step(i, fold_send.at[i - 1], fold_recv.at[i - 1], m_send, m_get)
        copy.start()
        m_copies.append(copy)
    matrix = fold(0)
    for copy in x_copies:
        copy.wait_recv()
    tokens = rows_all[...].reshape(seqs * rows, 2 * channels)
    latent_rows = tokens[:, :channels]
    token_scale = tokens[:, channels:channels + 1].astype(jnp.float32) + tokens[
        :, channels + channels // 2:channels + channels // 2 + 1
    ].astype(jnp.float32)
    for i in range(1, steps):
        m_copies[i - 1].wait_recv()
        matrix = matrix + fold_recv[i - 1].astype(jnp.float32)
    main = matrix[:channels]
    main_high = main.astype(jnp.bfloat16)
    main_low = (main - main_high.astype(jnp.float32)).astype(jnp.bfloat16)
    projected = token_scale * (
        jnp.dot(latent_rows, main_high, preferred_element_type=jnp.float32)
        + jnp.dot(latent_rows, main_low, preferred_element_type=jnp.float32)
    ) + matrix[channels:channels + 1]
    projected = projected.astype(jnp.bfloat16)
    queries = qk_norm(projected[:, :head_dim])
    keys = qk_norm(projected[:, head_dim:2 * head_dim])
    values = projected[:, 2 * head_dim:]
    last = (((1,), (1,)), ((), ()))
    scores = lax.dot_general(queries, keys, last, preferred_element_type=jnp.float32)
    weights = jnp.exp(scores * (1.0 / math.sqrt(head_dim)))
    probabilities = (weights / jnp.sum(weights, axis=-1, keepdims=True)).astype(jnp.bfloat16)
    attended = jnp.dot(probabilities, values, preferred_element_type=jnp.float32).astype(
        jnp.bfloat16
    )
    load_out.wait()
    share = lax.dot_general(attended, out_v[...], last, preferred_element_type=jnp.float32)
    for q in range(seqs):
        vel_send[q] = share[q * rows:(q + 1) * rows]
    v_copies = [
        to_seq(i, vel_send.at[seq_peer(i)], vel_recv.at[i - 1], v_send, v_get)
        for i in range(1, seqs)
    ]
    for copy in v_copies:
        copy.start()
    speed = vel_send[s]
    for i in range(1, seqs):
        v_copies[i - 1].wait_recv()
        speed = speed + vel_recv[i - 1]
    result[:, channels:] = speed

    step_size = (stamps[j + 1].astype(jnp.float32) - stamps[j].astype(jnp.float32)) * 0.001
    increment = step_size * speed + jnp.where(j == 0, lat_v[...], 0.0)
    result[:, :channels] = increment
    inc_send[...] = increment
    i_copies = [
        to_step(i, inc_send, inc_recv.at[i - 1], i_send, i_get) for i in range(1, steps)
    ]
    for i in range(1, steps):
        pl.when(j + i < steps)(i_copies[i - 1].start)
    for i in range(1, steps):
        @pl.when(j >= i)
        def _():
            i_copies[i - 1].wait_recv()
            result[:, :channels] += inc_recv[i - 1]

    for copy in (*a_copies, *x_copies, *b_copies, *m_copies, *v_copies):
        copy.wait_send()
    for i in range(1, steps):
        pl.when(j + i < steps)(i_copies[i - 1].wait_send)


def fused(steps, seqs, latents, timesteps, embed_weight, mod_weight, qkv_weight, out_weight):
    _, rows, channels = latents.shape
    width = embed_weight.shape[1]
    features = mod_weight.shape[0]
    block, _, _, head_dim = qkv_weight.shape
    lanes = block // seqs
    fold_rows = channels + 16
    bf16, f32 = jnp.bfloat16, jnp.float32
    out_shape = jax.ShapeDtypeStruct((rows, 2 * channels), f32)
    dma = pltpu.SemaphoreType.DMA
    seq_sems = [dma((seqs - 1,))] * 2
    step_sems = [dma((steps - 1,))] * 2
    result = pl.pallas_call(
        functools.partial(fused_kernel, steps, seqs),
        out_shape=pltpu.VMEM((rows, 2 * channels), f32),
        in_specs=[pl.BlockSpec(memory_space=pltpu.SMEM)] + [HBM] * 5,
        out_specs=VMEM,
        scratch_shapes=[
            pltpu.VMEM((rows, channels), f32),
            pltpu.VMEM((channels, width), bf16),
            pltpu.VMEM((2 * features, block), f32),
            pltpu.VMEM((block, 3 * head_dim), bf16),
            pltpu.VMEM((channels, head_dim), bf16),
            pltpu.VMEM((seqs, 2 * steps, lanes), f32),
            pltpu.VMEM((seqs - 1, 2 * steps, lanes), f32),
            pltpu.VMEM((seqs, 2 * steps, lanes), f32),
            pltpu.VMEM((seqs, rows, 2 * channels), bf16),
            pltpu.VMEM((channels, block), f32),
            pltpu.VMEM((steps * fold_rows, block), bf16),
            pltpu.VMEM((steps - 1, fold_rows, 3 * head_dim), bf16),
            pltpu.VMEM((steps - 1, fold_rows, 3 * head_dim), bf16),
            pltpu.VMEM((seqs, rows, channels), f32),
            pltpu.VMEM((seqs - 1, rows, channels), f32),
            pltpu.VMEM((rows, channels), f32),
            pltpu.VMEM((steps - 1, rows, channels), f32),
            dma((8,)),
            *seq_sems, *seq_sems, *seq_sems, *step_sems, *seq_sems, *step_sems,
        ],
        compiler_params=pltpu.CompilerParams(
            collective_id=0, has_side_effects=True, vmem_limit_bytes=56 * 1024 * 1024
        ),
    )(
        timesteps,
        latents[0],
        embed_weight,
        mod_weight,
        jnp.transpose(qkv_weight, (1, 2, 0, 3))[0],
        jnp.transpose(out_weight, (0, 2, 1))[0],
    )
    return result[None, :, :channels], result[None, :, channels:]


def body(steps, seqs, latents, timesteps, embed_weight, mod_weight, qkv_weight, out_weight):
    block, heads_here, _, head_dim = qkv_weight.shape
    fits = (
        steps > 1
        and seqs > 1
        and latents.shape[0] == 1
        and heads_here == 1
        and steps % 4 == 0
        and head_dim % 128 == 0
        and block % (seqs * 128) == 0
        and latents.shape[1] % 16 == 0
        and latents.shape[2] % 16 == 0
        and mod_weight.shape[0] % 8 == 0
    )
    run = functools.partial(fused, steps, seqs) if fits else on_device
    return run(latents, timesteps, embed_weight, mod_weight, qkv_weight, out_weight)


def solution(mesh):
    in_specs = (
        P("step", "seq", None),
        P(),
        P(),
        P("seq", None, None),
        P("step", "seq", None, None),
        P("seq", None, None),
    )
    out_specs = (P("step", "seq", None), P("step", "seq", None))
    return jax.shard_map(
        functools.partial(body, mesh.shape["step"], mesh.shape["seq"]), mesh=mesh, in_specs=in_specs, out_specs=out_specs, check_vma=False
    )
```

```python
import functools
import math

import jax
import jax.numpy as jnp
from jax import lax
from jax.experimental import pallas as pl
from jax.experimental.pallas import tpu as pltpu
from jax.sharding import PartitionSpec as P

FREQ = 256


def carried_in(shard, axis, combine, identity):
    devices, place = (lax.axis_size(axis), lax.axis_index(axis))
    everything = lax.all_gather(shard, axis)
    start = jnp.broadcast_to(jnp.asarray(identity, shard.dtype), shard.shape)

    def step(k, before):
        reached = k < place
        new = combine(before, everything[k])
        return jnp.where(reached, new, before)

    return lax.fori_loop(0, devices, step, start)


def condition_of(stamp):
    half_count = FREQ // 2
    frequencies = jnp.exp(
        -math.log(10000.0) * jnp.arange(half_count, dtype=jnp.float32) / half_count
    )
    angles = stamp * frequencies
    return jnp.concatenate([jnp.cos(angles), jnp.sin(angles)])


def modulate(latent_rows, embed_weight, shift_vec, scale_vec):
    embedded = jnp.dot(latent_rows, embed_weight, preferred_element_type=jnp.float32)
    center_mean = jnp.mean(embedded, axis=-1, keepdims=True)
    centered = embedded - center_mean
    variance = jnp.mean(centered * centered, axis=-1, keepdims=True)
    normed = centered * lax.rsqrt(variance + 1e-06)
    return (normed * (1.0 + scale_vec) + shift_vec).astype(jnp.bfloat16)


def qk_norm(head_rows):
    as_float = head_rows.astype(jnp.float32)
    return (
        as_float * lax.rsqrt(jnp.mean(as_float * as_float, axis=-1, keepdims=True) + 1e-06)
    ).astype(jnp.bfloat16)


def attend_head(head_block):
    queries = qk_norm(head_block[:, 0])
    key_rows = qk_norm(head_block[:, 1])
    values = head_block[:, 2]
    seq_length = queries.shape[0]
    head_dim = queries.shape[1]
    block_rows = math.gcd(seq_length, 512)
    query_blocks = queries.reshape(seq_length // block_rows, block_rows, head_dim)

    def one_block(query_block):
        scores = jnp.dot(query_block, key_rows.T, preferred_element_type=jnp.float32) * (
            1.0 / math.sqrt(head_dim)
        )
        weights = jnp.exp(scores)
        probabilities = (weights / jnp.sum(weights, axis=-1, keepdims=True)).astype(jnp.bfloat16)
        return jnp.dot(probabilities, values, preferred_element_type=jnp.float32).astype(
            jnp.bfloat16
        )

    return lax.map(one_block, query_blocks).reshape(seq_length, head_dim)


def add_terms(earlier_sum, later_sum):
    return earlier_sum + later_sum


def on_device(latents, timesteps, embed_weight, mod_weight, qkv_weight, out_weight):
    step_index = lax.axis_index("step")
    seq_index = lax.axis_index("seq")
    stamp_pair = lax.dynamic_slice_in_dim(timesteps, step_index, 2, 0).astype(jnp.float32)
    condition_vec = condition_of(stamp_pair[0])
    feature_rows = mod_weight.shape[0]
    local_features = lax.dynamic_slice_in_dim(
        condition_vec, seq_index * feature_rows, feature_rows, 0
    )
    partial_mod = jnp.einsum(
        "f,fcd->cd", local_features, mod_weight, precision=lax.Precision.HIGHEST
    )
    modulation = lax.psum(partial_mod, "seq")
    own_latents = latents[0].astype(jnp.bfloat16)
    all_latents = lax.all_gather(own_latents, "seq", axis=0, tiled=True)
    gathered = modulate(all_latents, embed_weight, modulation[0], modulation[1])
    seq_length = gathered.shape[0]
    heads_here = qkv_weight.shape[1]
    head_dim = qkv_weight.shape[3]
    qkv_width = heads_here * 3 * head_dim
    weight_piece = lax.all_gather(qkv_weight, "step", axis=0, tiled=True)
    flat_piece = weight_piece.reshape(weight_piece.shape[0], qkv_width)
    accumulated = jnp.dot(gathered, flat_piece, preferred_element_type=jnp.float32)
    projected = accumulated.astype(jnp.bfloat16).reshape(seq_length, heads_here, 3, head_dim)
    attended = lax.map(attend_head, jnp.moveaxis(projected, 1, 0))
    merged_heads = jnp.moveaxis(attended, 0, 1).reshape(seq_length, heads_here * head_dim)
    out_matrix = out_weight.reshape(heads_here * head_dim, out_weight.shape[2])
    velocity = lax.psum_scatter(
        jnp.dot(merged_heads, out_matrix, preferred_element_type=jnp.float32),
        "seq",
        scatter_dimension=0,
        tiled=True,
    )
    step_size = (stamp_pair[1] - stamp_pair[0]) / 1000.0
    increment = step_size * velocity + jnp.where(
        step_index == 0, latents[0], jnp.zeros_like(latents[0])
    )
    earlier = carried_in(increment, "step", add_terms, jnp.zeros_like(increment))
    updated = earlier + increment
    return (updated[None], velocity[None])


MESH = pl.DeviceIdType.MESH
HBM = pl.BlockSpec(memory_space=pltpu.HBM)
VMEM = pl.BlockSpec(memory_space=pltpu.VMEM)


def fused_kernel(
    steps, seqs, stamps_hbm, latents, embed_hbm, mod_hbm, qkv_hbm, out_hbm,
    result,
    stamps, lat_v, embed, mod_v, weight, out_v,
    mod_part, mod_recv, mod_all, rows_all, embed_own, lhs, fold_send, fold_recv,
    vel_send, vel_recv, inc_send, inc_recv,
    local_sem, a_send, a_get, b_send, b_get, x_send, x_get,
    m_send, m_get, v_send, v_get, i_send, i_get,
):
    j, s = lax.axis_index("step"), lax.axis_index("seq")
    rows, channels = lat_v.shape
    width = embed.shape[1]
    features = mod_hbm.shape[0]
    block = mod_v.shape[1]
    lanes = block // seqs
    fold_rows = fold_recv.shape[1]
    head_dim = out_v.shape[1]
    half = features * seqs // 2

    def seq_peer(i):
        return lax.rem(s + i, seqs)

    def step_peer(i):
        return lax.rem(j + i, steps)

    barrier = pltpu.get_barrier_semaphore()
    for i in range(1, seqs):
        pl.semaphore_signal(barrier, inc=1, device_id=(j, seq_peer(i)), device_id_type=MESH)
    for i in range(1, steps):
        pl.semaphore_signal(barrier, inc=1, device_id=(step_peer(i), s), device_id_type=MESH)

    own_columns = pl.ds(pl.multiple_of(j * block, block), block)
    loads = [
        pltpu.make_async_copy(
            mod_hbm.at[:, c, own_columns],
            mod_v.at[pl.ds(c * features, features), :],
            local_sem.at[c],
        )
        for c in range(2)
    ]
    load_lat = pltpu.make_async_copy(latents, lat_v, local_sem.at[2])
    load_embed = pltpu.make_async_copy(embed_hbm, embed, local_sem.at[3])
    load_weight = [
        pltpu.make_async_copy(
            qkv_hbm.at[c], weight.at[:, pl.ds(c * head_dim, head_dim)], local_sem.at[4 + c]
        )
        for c in range(3)
    ]
    load_stamps = pltpu.make_async_copy(stamps_hbm, stamps, local_sem.at[8])
    load_out = pltpu.make_async_copy(out_hbm, out_v, local_sem.at[7])
    for copy in (load_stamps, *loads, load_lat, load_embed, *load_weight, load_out):
        copy.start()

    shape = (2 * steps, 2 * features)
    row = lax.broadcasted_iota(jnp.int32, shape, 0)
    column = lax.broadcasted_iota(jnp.int32, shape, 1)
    low_row, low_column = row < steps, column < features
    step_of = jnp.where(low_row, row, row - steps)
    feature = jnp.where(low_column, column, column - features) + s * features
    is_cos = feature < half
    index = jnp.where(is_cos, feature, feature - half)
    stamp = jnp.zeros(shape, jnp.float32)
    load_stamps.wait()
    for k in range(steps):
        stamp = jnp.where(step_of == k, stamps[k].astype(jnp.float32), stamp)
    frequency = jnp.exp(-math.log(10000.0) * index.astype(jnp.float32) / half)
    angle = stamp * frequency
    condition = jnp.where(is_cos, jnp.cos(angle), jnp.sin(angle))
    condition = jnp.where(low_row == low_column, condition, 0.0)

    for copy in loads:
        copy.wait()
    part = jnp.dot(
        condition, mod_v[...], precision=lax.Precision.HIGHEST, preferred_element_type=jnp.float32
    )
    for q in range(seqs):
        mod_part[q] = part[:, q * lanes:(q + 1) * lanes]

    pl.semaphore_wait(barrier, seqs + steps - 2)

    def to_seq(i, src, dst, send, get):
        return pltpu.make_async_remote_copy(
            src_ref=src, dst_ref=dst, send_sem=send.at[i - 1], recv_sem=get.at[i - 1],
            device_id=(j, seq_peer(i)), device_id_type=MESH,
        )

    def to_step(i, src, dst, send, get):
        return pltpu.make_async_remote_copy(
            src_ref=src, dst_ref=dst, send_sem=send.at[i - 1], recv_sem=get.at[i - 1],
            device_id=(step_peer(i), s), device_id_type=MESH,
        )

    a_copies = [
        to_seq(i, mod_part.at[seq_peer(i)], mod_recv.at[i - 1], a_send, a_get)
        for i in range(1, seqs)
    ]
    for copy in a_copies:
        copy.start()

    load_lat.wait()
    load_embed.wait()
    own = lat_v[...].astype(jnp.bfloat16)
    embedded = jnp.dot(own, embed[...], preferred_element_type=jnp.float32)
    centered = embedded - jnp.mean(embedded, axis=-1, keepdims=True)
    scale = lax.rsqrt(jnp.mean(centered * centered, axis=-1, keepdims=True) + 1e-06)
    scale_high = scale.astype(jnp.bfloat16)
    scale_low = (scale - scale_high.astype(jnp.float32)).astype(jnp.bfloat16)
    rows_all[s] = jnp.concatenate(
        [
            own,
            jnp.broadcast_to(scale_high, (rows, channels // 2)),
            jnp.broadcast_to(scale_low, (rows, channels // 2)),
        ],
        axis=1,
    )

    total = mod_part[s]
    for i in range(1, seqs):
        a_copies[i - 1].wait_recv()
        total = total + mod_recv[i - 1]
    mod_all[s] = total
    b_copies = [
        to_seq(i, mod_all.at[s], mod_all.at[s], b_send, b_get) for i in range(1, seqs)
    ]
    for copy in b_copies:
        copy.start()
    x_copies = [
        to_seq(i, rows_all.at[s], rows_all.at[s], x_send, x_get) for i in range(1, seqs)
    ]
    for copy in x_copies:
        copy.start()

    embed_mean = jnp.mean(embed[...].astype(jnp.float32), axis=-1, keepdims=True)
    embed_own[...] = embed[:, own_columns].astype(jnp.float32) - embed_mean
    tail_row = lax.broadcasted_iota(jnp.int32, (fold_rows - channels, lanes), 0)
    for copy in b_copies:
        copy.wait_recv()
    for copy in load_weight:
        copy.wait()

    def fold(i):
        k = step_peer(i)
        for q in range(seqs):
            at = pl.ds(q * lanes, lanes)
            shift_k = mod_all[q, pl.ds(k, 1), :]
            scale_k = mod_all[q, pl.ds(steps + k, 1), :]
            lhs[pl.ds(i * fold_rows, channels), at] = (
                embed_own[:, at] * (1.0 + scale_k)
            ).astype(jnp.bfloat16)
            lhs[pl.ds(i * fold_rows + channels, fold_rows - channels), at] = jnp.where(
                tail_row == 0, shift_k, 0.0
            ).astype(jnp.bfloat16)
        return jnp.dot(
            lhs[pl.ds(i * fold_rows, fold_rows), :], weight[...],
            preferred_element_type=jnp.float32,
        )

    m_copies = []
    for i in range(1, steps):
        fold_send[i - 1] = fold(i).astype(jnp.bfloat16)
        copy = to_step(i, fold_send.at[i - 1], fold_recv.at[i - 1], m_send, m_get)
        copy.start()
        m_copies.append(copy)
    matrix = fold(0)
    for copy in x_copies:
        copy.wait_recv()
    tokens = rows_all[...].reshape(seqs * rows, 2 * channels)
    latent_rows = tokens[:, :channels]
    token_scale = tokens[:, channels:channels + 1].astype(jnp.float32) + tokens[
        :, channels + channels // 2:channels + channels // 2 + 1
    ].astype(jnp.float32)
    for i in range(1, steps):
        m_copies[i - 1].wait_recv()
        matrix = matrix + fold_recv[i - 1].astype(jnp.float32)
    main = matrix[:channels]
    main_high = main.astype(jnp.bfloat16)
    main_low = (main - main_high.astype(jnp.float32)).astype(jnp.bfloat16)
    projected = token_scale * (
        jnp.dot(latent_rows, main_high, preferred_element_type=jnp.float32)
        + jnp.dot(latent_rows, main_low, preferred_element_type=jnp.float32)
    ) + matrix[channels:channels + 1]
    projected = projected.astype(jnp.bfloat16)
    queries = qk_norm(projected[:, :head_dim])
    keys = qk_norm(projected[:, head_dim:2 * head_dim])
    values = projected[:, 2 * head_dim:]
    last = (((1,), (1,)), ((), ()))
    scores = lax.dot_general(queries, keys, last, preferred_element_type=jnp.float32)
    weights = jnp.exp(scores * (1.0 / math.sqrt(head_dim)))
    probabilities = (weights / jnp.sum(weights, axis=-1, keepdims=True)).astype(jnp.bfloat16)
    attended = jnp.dot(probabilities, values, preferred_element_type=jnp.float32).astype(
        jnp.bfloat16
    )
    load_out.wait()
    share = lax.dot_general(attended, out_v[...], last, preferred_element_type=jnp.float32)
    for q in range(seqs):
        vel_send[q] = share[q * rows:(q + 1) * rows]
    v_copies = [
        to_seq(i, vel_send.at[seq_peer(i)], vel_recv.at[i - 1], v_send, v_get)
        for i in range(1, seqs)
    ]
    for copy in v_copies:
        copy.start()
    speed = vel_send[s]
    for i in range(1, seqs):
        v_copies[i - 1].wait_recv()
        speed = speed + vel_recv[i - 1]
    result[:, channels:] = speed

    step_size = (stamps[j + 1].astype(jnp.float32) - stamps[j].astype(jnp.float32)) * 0.001
    increment = step_size * speed + jnp.where(j == 0, lat_v[...], 0.0)
    result[:, :channels] = increment
    inc_send[...] = increment
    i_copies = [
        to_step(i, inc_send, inc_recv.at[i - 1], i_send, i_get) for i in range(1, steps)
    ]
    for i in range(1, steps):
        pl.when(j + i < steps)(i_copies[i - 1].start)
    for i in range(1, steps):
        @pl.when(j >= i)
        def _():
            i_copies[i - 1].wait_recv()
            result[:, :channels] += inc_recv[i - 1]

    for copy in (*a_copies, *x_copies, *b_copies, *m_copies, *v_copies):
        copy.wait_send()
    for i in range(1, steps):
        pl.when(j + i < steps)(i_copies[i - 1].wait_send)


def fused(steps, seqs, latents, timesteps, embed_weight, mod_weight, qkv_weight, out_weight):
    _, rows, channels = latents.shape
    width = embed_weight.shape[1]
    features = mod_weight.shape[0]
    block, _, _, head_dim = qkv_weight.shape
    lanes = block // seqs
    fold_rows = channels + 16
    bf16, f32 = jnp.bfloat16, jnp.float32
    out_shape = jax.ShapeDtypeStruct((rows, 2 * channels), f32)
    dma = pltpu.SemaphoreType.DMA
    seq_sems = [dma((seqs - 1,))] * 2
    step_sems = [dma((steps - 1,))] * 2
    result = pl.pallas_call(
        functools.partial(fused_kernel, steps, seqs),
        out_shape=pltpu.VMEM((rows, 2 * channels), f32),
        in_specs=[HBM] * 6,
        out_specs=VMEM,
        scratch_shapes=[
            pltpu.SMEM(timesteps.shape, jnp.int32),
            pltpu.VMEM((rows, channels), f32),
            pltpu.VMEM((channels, width), bf16),
            pltpu.VMEM((2 * features, block), f32),
            pltpu.VMEM((block, 3 * head_dim), bf16),
            pltpu.VMEM((channels, head_dim), bf16),
            pltpu.VMEM((seqs, 2 * steps, lanes), f32),
            pltpu.VMEM((seqs - 1, 2 * steps, lanes), f32),
            pltpu.VMEM((seqs, 2 * steps, lanes), f32),
            pltpu.VMEM((seqs, rows, 2 * channels), bf16),
            pltpu.VMEM((channels, block), f32),
            pltpu.VMEM((steps * fold_rows, block), bf16),
            pltpu.VMEM((steps - 1, fold_rows, 3 * head_dim), bf16),
            pltpu.VMEM((steps - 1, fold_rows, 3 * head_dim), bf16),
            pltpu.VMEM((seqs, rows, channels), f32),
            pltpu.VMEM((seqs - 1, rows, channels), f32),
            pltpu.VMEM((rows, channels), f32),
            pltpu.VMEM((steps - 1, rows, channels), f32),
            dma((9,)),
            *seq_sems, *seq_sems, *seq_sems, *step_sems, *seq_sems, *step_sems,
        ],
        compiler_params=pltpu.CompilerParams(
            collective_id=0, has_side_effects=True, vmem_limit_bytes=56 * 1024 * 1024
        ),
    )(
        timesteps,
        latents[0],
        embed_weight,
        mod_weight,
        jnp.transpose(qkv_weight, (1, 2, 0, 3))[0],
        jnp.transpose(out_weight, (0, 2, 1))[0],
    )
    return result[None, :, :channels], result[None, :, channels:]


def body(steps, seqs, latents, timesteps, embed_weight, mod_weight, qkv_weight, out_weight):
    block, heads_here, _, head_dim = qkv_weight.shape
    fits = (
        steps > 1
        and seqs > 1
        and latents.shape[0] == 1
        and heads_here == 1
        and steps % 4 == 0
        and head_dim % 128 == 0
        and block % (seqs * 128) == 0
        and latents.shape[1] % 16 == 0
        and latents.shape[2] % 16 == 0
        and mod_weight.shape[0] % 8 == 0
    )
    run = functools.partial(fused, steps, seqs) if fits else on_device
    return run(latents, timesteps, embed_weight, mod_weight, qkv_weight, out_weight)


def solution(mesh):
    in_specs = (
        P("step", "seq", None),
        P(),
        P(),
        P("seq", None, None),
        P("step", "seq", None, None),
        P("seq", None, None),
    )
    out_specs = (P("step", "seq", None), P("step", "seq", None))
    return jax.shard_map(
        functools.partial(body, mesh.shape["step"], mesh.shape["seq"]), mesh=mesh, in_specs=in_specs, out_specs=out_specs, check_vma=False
    )
```
